256 devices in a mesh: row: 16 (over x, y_hi, core), col: 16 (over z, y_lo).
Axes of the slice: x: 4, y: 4 (y_hi: 2, y_lo: 2; y = y_hi * 2 + y_lo), z: 8, core: 2. Of those that a mesh axis runs over, the one named last changes fastest.
Arguments:
- features: float32 [65536, 128], P(('row', 'col')), may hold values from -6 to 6
- weight: float32 [128, 256], replicated, may hold values from -2 to 2
- offset: float32 [256], replicated, may hold values from -3 to 3
- cotangent: float32 [65536, 256], P(('row', 'col')), may hold values from -6 to 6
- tile_index: int32 [16, 16, 2, 32], P('row', 'col'), may hold values from 0 to 15, as said below
- edge_mask: int32 [16, 16, 32, 256, 256], P('row', 'col'), may hold values from 0 to 1, as said below
Outputs:
- hidden: float32 [65536, 256], P(('row', 'col'))
- grad_features: float32 [65536, 128], P(('row', 'col'))
- grad_weight: float32 [128, 256], replicated
- grad_offset: float32 [256], replicated
The draws below stay inside these ranges and needn't reach their ends.
Inputs may be any that keep to these rules, and one draw needn't show every extreme that they name: `tile_index`: on each device the listed tiles are distinct and come first in its slots; a device lists 32, 16, 8 or 4 tiles and at least one device lists 32; the slots after the listed ones name block 0 of both slabs. The first entry counts block rows of the row slab, the second block columns of the column slab. `edge_mask`: slots after a device's listed tiles hold only zeros.
All inputs are finite; a program needn't handle non-finite values.
Results may differ from the reference program's by a relative error of at most 0.0003.
Values sent between devices are 32-bit elements; how exact they have to be, the bound alone decides.
No kernel may reach another device: no remote copies, remote signals or barrier semaphores. Data moves between devices by JAX's collectives and lax.ppermute only.
A program may use at most 128 MiB of HBM per device.

```python
import jax
import jax.numpy as jnp
from jax import lax

F = 128
H = 256
TILE = 256
GROUP = 256
TMAX = 32
NODES = 65536
N_ROW = 16
N_COL = 16


def tile_layout(key):
    key = jax.random.fold_in(key, 11)
    device_total = N_ROW * N_COL
    col_blocks = N_ROW * GROUP // TILE
    places = N_COL * GROUP // TILE * col_blocks
    device_keys = jax.random.split(jax.random.fold_in(key, 1), device_total)
    orders = jax.vmap(lambda single: jax.random.permutation(single, places)[:TMAX])(device_keys).astype(jnp.int32)
    shifts = jax.random.randint(jax.random.fold_in(key, 2), (device_total,), 0, 4).astype(jnp.int32)
    listed = jnp.right_shift(jnp.full((device_total,), TMAX, jnp.int32), shifts)
    fullest = jax.random.randint(jax.random.fold_in(key, 3), (), 0, device_total).astype(jnp.int32)
    listed = jnp.where(jnp.arange(device_total, dtype=jnp.int32) == fullest, TMAX, listed)
    live_slots = jnp.arange(TMAX, dtype=jnp.int32)[None, :] < listed[:, None]
    orders = jnp.where(live_slots, orders, 0)
    return (orders, live_slots)


def draw_tile_index(key, part):
    orders, live_slots = tile_layout(key)
    col_blocks = N_ROW * GROUP // TILE
    block_row = orders // col_blocks
    block_col = orders % col_blocks
    stacked = jnp.stack([block_row, block_col], axis=1)
    return stacked.reshape(N_ROW, N_COL, 2, TMAX).astype(jnp.int32)


def draw_edge_mask(key, part):
    orders, live_slots = tile_layout(key)
    key = jax.random.fold_in(key, 5)
    device_total = N_ROW * N_COL
    levels = jax.random.randint(jax.random.fold_in(key, 1), (device_total, TMAX, 1, 1), 1, 9)
    tickets = jax.random.randint(jax.random.fold_in(key, 2), (device_total, TMAX, TILE, TILE), 0, 4 * TILE)
    present = jnp.logical_and(tickets < levels, live_slots[:, :, None, None])
    return present.astype(jnp.int32).reshape(N_ROW, N_COL, TMAX, TILE, TILE)


def block_scale(rng, extent, cuts, smallest, high):
    gain = 1.0
    for axis_at, parts in cuts:
        steps = jax.random.uniform(jax.random.fold_in(jax.random.fold_in(rng, 6), axis_at), (parts,), jnp.float32, smallest / len(cuts), high / len(cuts))
        gain = gain * jnp.repeat(jnp.exp(steps), extent[axis_at] // parts).reshape((-1,) + (1,) * (len(extent) - 1 - axis_at))
    return gain


def noise(rng, dims, spread, most, shards=(), held_as=jnp.bfloat16):
    level = block_scale(rng, dims, shards, -0.22, 0.18) if shards else 1.0
    result = jax.random.normal(rng, dims, jnp.float32) * spread * level
    return jnp.minimum(jnp.maximum(result, -most), most).astype(held_as)


def setup_inputs(seed: int = 0) -> dict:
    splits = jax.random.split(jax.random.key(seed), 7)
    return {
        "features": noise(splits[0], (NODES, F), 1.0, 6.0, ((0, 256),), jnp.float32),
        "weight": noise(splits[1], (F, H), (F // 16) ** -0.5, 2.0, (), jnp.float32),
        "offset": noise(splits[2], (H,), 0.5, 3.0, (), jnp.float32),
        "cotangent": noise(splits[3], (NODES, H), 1.0, 6.0, ((0, 256),), jnp.float32),
        "tile_index": draw_tile_index(jax.random.fold_in(splits[6], 71), 0),
        "edge_mask": draw_edge_mask(jax.random.fold_in(splits[6], 71), 0),
    }


highest = lax.Precision.HIGHEST

def gaussian_unit(values):
    return 0.5 * values * (1.0 + lax.erf(values * 0.7071067811865476))

def gaussian_slope(values):
    return 0.5 * (1.0 + lax.erf(values * 0.7071067811865476)) + values * jnp.exp(-0.5 * values * values) * 0.3989422804014327

def reference(features, weight, offset, cotangent, tile_index, edge_mask):
    row_blocks = N_COL * GROUP // TILE
    col_blocks = N_ROW * GROUP // TILE
    grid_rows = features.reshape(N_ROW, N_COL, GROUP, F)
    column_slabs = jnp.transpose(grid_rows, (1, 0, 2, 3)).reshape(N_COL, col_blocks, TILE, F)
    flat_index = tile_index.reshape(N_ROW * N_COL, 2, TMAX)
    flat_mask = edge_mask.reshape(N_ROW * N_COL, TMAX, TILE, TILE)
    block_rows = jnp.arange(row_blocks, dtype=jnp.int32)
    block_cols = jnp.arange(col_blocks, dtype=jnp.int32)
    devices = jnp.arange(N_ROW * N_COL, dtype=jnp.int32)

    def forward_step(carry, device):
        sums, counts = carry
        row_pos = device // N_COL
        col_pos = device % N_COL
        edge_values = flat_mask[device].astype(jnp.float32)
        picked = column_slabs[col_pos][flat_index[device, 1]]
        products = jnp.einsum('tuv,tvf->tuf', edge_values, picked, precision=highest)
        onehot = (block_rows[:, None] == flat_index[device, 0][None, :]).astype(jnp.float32)
        sums = sums.at[row_pos].add(jnp.einsum('pt,tuf->puf', onehot, products, precision=highest))
        counts = counts.at[row_pos].add(jnp.einsum('pt,tu->pu', onehot, lax.optimization_barrier(jnp.sum(edge_values, axis=2)), precision=highest))
        return ((sums, counts), None)
    start = (jnp.zeros((N_ROW, row_blocks, TILE, F), jnp.float32), jnp.zeros((N_ROW, row_blocks, TILE), jnp.float32))
    (sums, counts), _ = lax.scan(forward_step, start, devices)
    degree = 1.0 + counts.reshape(NODES)
    aggregated = (sums.reshape(NODES, F) + features) / degree[:, None]
    activation_in = jnp.dot(aggregated, weight, precision=highest, preferred_element_type=jnp.float32) + offset
    hidden = gaussian_unit(activation_in)
    grad_pre = cotangent * gaussian_slope(activation_in)
    outgoing = jnp.dot(grad_pre, weight.T, precision=highest, preferred_element_type=jnp.float32) / degree[:, None]
    row_slabs = outgoing.reshape(N_ROW, row_blocks, TILE, F)

    def backward_step(totals, device):
        row_pos = device // N_COL
        col_pos = device % N_COL
        edge_values = flat_mask[device].astype(jnp.float32)
        picked = row_slabs[row_pos][flat_index[device, 0]]
        products = jnp.einsum('tuv,tuf->tvf', edge_values, picked, precision=highest)
        onehot = (block_cols[:, None] == flat_index[device, 1][None, :]).astype(jnp.float32)
        totals = totals.at[col_pos].add(jnp.einsum('pt,tvf->pvf', onehot, products, precision=highest))
        return (totals, None)
    totals, _ = lax.scan(backward_step, jnp.zeros((N_COL, col_blocks, TILE, F), jnp.float32), devices)
    back_nodes = jnp.transpose(totals.reshape(N_COL, N_ROW, GROUP, F), (1, 0, 2, 3)).reshape(NODES, F)
    grad_features = back_nodes + outgoing
    factor = 1.0 / jnp.sqrt(jnp.asarray(NODES, jnp.float32))
    grad_weight = jnp.dot(aggregated.T, grad_pre, precision=highest, preferred_element_type=jnp.float32) * factor
    grad_offset = lax.optimization_barrier(jnp.sum(grad_pre, axis=0)) * factor
    return (hidden, grad_features, grad_weight, grad_offset)
```

```python
import functools

import jax
import jax.numpy as jnp
import numpy as np
from jax import lax
from jax.experimental import pallas as pl
from jax.experimental.pallas import tpu as pltpu
from jax.sharding import Mesh
from jax.sharding import PartitionSpec as P

SIZES = {"x": 4, "yh": 2, "core": 2, "z": 8, "yl": 2}
AXES = tuple(SIZES)
F = 128
H = 256
TILE = 256
TMAX = 32
BLOCKS = 16
COUNT = 8
BLOCK = F + COUNT
PIECE = 16
STEP = 4
highest = lax.Precision.HIGHEST
f32 = jnp.float32
bf16 = jnp.bfloat16


def shift(value, axis, by):
    size = SIZES[axis]
    return lax.ppermute(value, axis, [(i, (i + by) % size) for i in range(size)])


def whole(shape):
    return pl.BlockSpec(shape, lambda *_: (0,) * len(shape))


def params(mib):
    return pltpu.CompilerParams(vmem_limit_bytes=mib * 1024 * 1024)


def split_terms(values):
    high = values.astype(bf16)
    return high, (values - high.astype(f32)).astype(bf16)


def narrow_body(mask_ref, out_ref):
    out_ref[...] = mask_ref[...].astype(f32).astype(bf16)


def narrow_mask(mask):
    spec = pl.BlockSpec((STEP, TILE, TILE), lambda t: (t, 0, 0))
    return pl.pallas_call(
        narrow_body,
        grid=(TMAX // STEP,),
        in_specs=[spec],
        out_specs=spec,
        out_shape=jax.ShapeDtypeStruct((TMAX, TILE, TILE), bf16),
        compiler_params=params(16),
        cost_estimate=pl.CostEstimate(
            flops=TMAX * TILE * TILE, bytes_accessed=6 * TMAX * TILE * TILE, transcendentals=0
        ),
    )(mask)


def source_slot(block):
    x, yh, core = block >> 2, (block >> 1) & 1, block & 1
    x_rel = (x - lax.axis_index("x")) & 3
    yh_rel = yh ^ lax.axis_index("yh")
    core_rel = core ^ lax.axis_index("core")
    return core_rel * 8 + x_rel * 2 + yh_rel


def target_slot(block):
    z, yl = block >> 1, block & 1
    return ((z - lax.axis_index("z")) & 7) * 2 + (yl ^ lax.axis_index("yl"))


def forward_body(index_ref, mask_ref, *refs):
    sources, (out_ref, held) = refs[:16], refs[16:]
    step = pl.program_id(0)

    @pl.when(step == 0)
    def _():
        for slot in range(BLOCKS):
            high, low = split_terms(sources[slot][...])
            held[slot, :F, :] = high
            held[slot, F : 2 * F, :] = low
            held[slot, 2 * F :, :] = jnp.ones((16, TILE), bf16)
        out_ref[...] = jnp.zeros_like(out_ref)

    for k in range(STEP):
        tile = step * STEP + k
        target = target_slot(index_ref[0, tile])
        source = source_slot(index_ref[1, tile])
        product = lax.dot_general(
            held[source], mask_ref[k], (((1,), (1,)), ((), ())), preferred_element_type=f32
        )
        out_ref[target, :F, :] += product[:F] + product[F : 2 * F]
        out_ref[target, F:, :] += product[2 * F : 2 * F + COUNT]


def forward_products(index, mask, sources):
    return pl.pallas_call(
        forward_body,
        grid=(TMAX // STEP,),
        in_specs=[
            pl.BlockSpec(memory_space=pltpu.SMEM),
            pl.BlockSpec((STEP, TILE, TILE), lambda t: (t, 0, 0)),
        ]
        + [whole((F, TILE))] * BLOCKS,
        out_specs=whole((BLOCKS, BLOCK, TILE)),
        out_shape=jax.ShapeDtypeStruct((BLOCKS, BLOCK, TILE), f32),
        scratch_shapes=[pltpu.VMEM((BLOCKS, 2 * F + 16, TILE), bf16)],
        compiler_params=params(32),
        cost_estimate=pl.CostEstimate(
            flops=4 * TMAX * TILE * TILE * F, bytes_accessed=2 * TMAX * TILE * TILE, transcendentals=0
        ),
    )(index, mask, *sources)


def dense_body(a_ref, b_ref, c_ref, d_ref, x_ref, w_ref, o_ref, g_ref, hidden_ref, out_ref, gw_ref):
    total = a_ref[...] + b_ref[...] + c_ref[...] + d_ref[...]
    degree = 1.0 + total[F : F + 1]
    aggregated = (total[:F] + x_ref[...]) / degree
    weight = w_ref[...]
    active = (
        jnp.dot(aggregated.T, weight, precision=highest, preferred_element_type=f32) + o_ref[...]
    )
    bell = 1.0 + lax.erf(active * 0.7071067811865476)
    hidden_ref[...] = 0.5 * active * bell
    slope = 0.5 * bell + active * jnp.exp(-0.5 * active * active) * 0.3989422804014327
    grad_pre = g_ref[...] * slope
    out_ref[...] = (
        lax.dot_general(
            weight, grad_pre, (((1,), (1,)), ((), ())), precision=highest, preferred_element_type=f32
        )
        / degree
    )
    grad_weight = jnp.dot(aggregated, grad_pre, precision=highest, preferred_element_type=f32)
    offset = jnp.broadcast_to(jnp.sum(grad_pre, axis=0, keepdims=True), (8, H))
    for k in range(BLOCKS):
        gw_ref[k, :8, :] = grad_weight[8 * k : 8 * k + 8]
        gw_ref[k, 8:, :] = offset


def dense(parts, x_t, weight, offset, cotangent):
    return pl.pallas_call(
        dense_body,
        out_shape=(
            jax.ShapeDtypeStruct((TILE, H), f32),
            jax.ShapeDtypeStruct((F, TILE), f32),
            jax.ShapeDtypeStruct((BLOCKS, PIECE, H), f32),
        ),
        compiler_params=params(32),
    )(*parts, x_t, weight, offset.reshape(1, H), cotangent)


def backward_body(index_ref, mask_ref, *refs):
    ins, (near_ref, far_ref, held, sums) = refs[:9], refs[9:]
    step = pl.program_id(0)
    places = [(0, 0), (7, 1), (1, 2), (6, 3), (2, 4), (5, 5), (3, 6)]
    parts = [(2 * z + h, ins[k], h * (F + PIECE)) for z, k in places for h in range(2)]
    parts += [(8, ins[7], 0), (9, ins[8], 0)]

    @pl.when(step == 0)
    def _():
        for slot, ref, start in parts:
            high, low = split_terms(ref[start : start + F, :])
            held[slot, :F, :] = high
            held[slot, F:, :] = low
        sums[...] = jnp.zeros_like(sums)

    for k in range(STEP):
        tile = step * STEP + k
        source = target_slot(index_ref[0, tile])
        target = source_slot(index_ref[1, tile])
        product = jnp.dot(held[source], mask_ref[k], preferred_element_type=f32)
        sums[target] += product[:F] + product[F:]

    @pl.when(step == TMAX // STEP - 1)
    def _():
        piece = jnp.zeros((PIECE, H), f32)
        for slot, ref, start in parts:
            piece = piece + ref[start + F : start + F + PIECE, :]
        for slot in range(8):
            near_ref[slot * F : (slot + 1) * F, :] = sums[slot]
            far_ref[slot * F : (slot + 1) * F, :] = sums[8 + slot]
        near_ref[8 * F :, :] = piece
        far_ref[8 * F :, :] = piece


def backward_products(index, mask, gathered):
    rows = 8 * F + PIECE
    return pl.pallas_call(
        backward_body,
        grid=(TMAX // STEP,),
        in_specs=[
            pl.BlockSpec(memory_space=pltpu.SMEM),
            pl.BlockSpec((STEP, TILE, TILE), lambda t: (t, 0, 0)),
        ]
        + [whole(value.shape) for value in gathered],
        out_specs=(whole((rows, TILE)), whole((rows, TILE))),
        out_shape=(jax.ShapeDtypeStruct((rows, TILE), f32),) * 2,
        scratch_shapes=[
            pltpu.VMEM((BLOCKS, 2 * F, TILE), bf16),
            pltpu.VMEM((BLOCKS, F, TILE), f32),
        ],
        compiler_params=params(32),
        cost_estimate=pl.CostEstimate(
            flops=4 * TMAX * TILE * TILE * F, bytes_accessed=2 * TMAX * TILE * TILE, transcendentals=0
        ),
    )(index, mask, *gathered)


def final_body(scale, near_ref, other_ref, out_ref, pieces_ref, yonder_ref, grad_ref, gw_ref, go_ref):
    grad_ref[...] = (near_ref[...] + other_ref[:F, :] + out_ref[...]).T
    x, yh, core = (lax.axis_index(a) for a in ("x", "yh", "core"))
    for h, ref, start in ((0, pieces_ref, 0), (1, yonder_ref, F)):
        for k, by in enumerate((0, 3, 1, 2)):
            for c in range(2):
                block = ((x + by) & 3) * 4 + (yh ^ h) * 2 + (core ^ c)
                at = start + (k * 2 + c) * PIECE
                gw_ref[pl.ds(pl.multiple_of(block * 8, 8), 8), :] = ref[at : at + 8, :] * scale
    go_ref[...] = pieces_ref[8:16, :] * scale


def finish(near, other, outgoing, pieces, scale):
    return pl.pallas_call(
        functools.partial(final_body, scale),
        out_shape=(
            jax.ShapeDtypeStruct((TILE, F), f32),
            jax.ShapeDtypeStruct((F, H), f32),
            jax.ShapeDtypeStruct((8, H), f32),
        ),
        compiler_params=params(16),
    )(near, other, outgoing, pieces, other)


def gather_row(x_t):
    h = shift(x_t, "yh", 1)
    r1, l1 = shift(x_t, "x", 1), shift(x_t, "x", -1)
    r1h, l1h = shift(h, "x", 1), shift(h, "x", -1)
    r2, l2 = shift(r1, "x", 1), shift(l1h, "x", -1)
    own = [x_t, h, l1, l1h, r2, l2, r1, r1h]
    pairs = [[x_t, h], [l1, r1], [l1h, r1h], [r2, l2]]
    far = []
    for a, b in pairs:
        both = shift(jnp.concatenate([a, b], axis=0), "core", 1)
        far.append((both[:F], both[F:]))
    (f0, f1), (f2, f6), (f3, f7), (f4, f5) = far
    return own + [f0, f1, f2, f3, f4, f5, f6, f7]


def scatter_col(sums):
    two = lambda z: sums[2 * (z % 8) : 2 * (z % 8) + 2].reshape(2 * BLOCK, TILE)
    right, left = shift(sums[8], "z", 1), shift(sums[9], "z", -1)
    right = two(3).at[:BLOCK].add(right)
    left = two(-3).at[BLOCK:].add(left)
    right, left = shift(right, "z", 1), shift(left, "z", -1)
    right, left = shift(right + two(2), "z", 1), shift(left + two(-2), "z", -1)
    right, left = shift(right + two(1), "z", 1), shift(left + two(-1), "z", -1)
    other = shift(right[BLOCK:] + left[BLOCK:] + sums[1], "yl", 1)
    return sums[0], right[:BLOCK], left[:BLOCK], other


def gather_col(value):
    half = value.shape[0]
    both = jnp.concatenate([value, shift(value, "yl", 1)], axis=0)
    r1, l1 = shift(both, "z", 1), shift(both, "z", -1)
    r2, l2 = shift(r1, "z", 1), shift(l1, "z", -1)
    r3, l3 = shift(r2, "z", 1), shift(l2, "z", -1)
    r4, l4 = shift(r3[:half], "z", 1), shift(l3[half:], "z", -1)
    return both, r1, l1, r2, l2, r3, l3, r4, l4


def scatter_row(near, far):
    got = shift(far, "core", 1)
    total = near[: 8 * F] + got[: 8 * F]
    pieces = jnp.concatenate([near[8 * F :], got[8 * F :]], axis=0)
    two = lambda x: total[x % 4 * 2 * F : (x % 4 * 2 + 2) * F]
    right = shift(jnp.concatenate([two(2)[:F], pieces], axis=0), "x", 1)
    left = shift(jnp.concatenate([two(2)[F:], pieces], axis=0), "x", -1)
    from_left, from_right = right[F:], left[F:]
    right = jnp.concatenate([two(1).at[:F].add(right[:F]), from_left], axis=0)
    left = two(-1).at[F:].add(left[:F])
    right, left = shift(right, "x", 1), shift(left, "x", -1)
    mine = two(0) + right[: 2 * F] + left
    pieces = jnp.concatenate([pieces, from_left, from_right, right[2 * F :]], axis=0)
    other = shift(jnp.concatenate([mine[F:], pieces], axis=0), "yh", 1)
    return mine[:F], other, pieces


def per_device(features, weight, offset, cotangent, tile_index, edge_mask):
    index = tile_index.reshape(2, TMAX)
    x_t = features.T
    sources = gather_row(x_t)
    mask = narrow_mask(edge_mask.reshape(TMAX, TILE, TILE))
    sums = forward_products(index, mask, sources)
    parts = scatter_col(sums)
    hidden, outgoing, gw = dense(parts, x_t, weight, offset, cotangent)
    spread = lax.all_to_all(gw, ("x", "yh", "core"), 0, 0, tiled=True)
    piece = jnp.sum(spread, axis=0)
    gathered = gather_col(jnp.concatenate([outgoing, piece], axis=0))
    near, far = backward_products(index, mask, gathered)
    mine, other, pieces = scatter_row(near, far)
    scale = 1.0 / float(np.sqrt(BLOCKS * BLOCKS * TILE))
    grad, grad_weight, grad_offset = finish(mine, other, outgoing, pieces, scale)
    return hidden, grad, grad_weight, grad_offset[0]


def solution(mesh):
    fine = Mesh(mesh.devices.reshape(tuple(SIZES.values())), AXES)
    row, col = ("x", "yh", "core"), ("z", "yl")
    nodes = P(row + col, None)
    return jax.shard_map(
        per_device,
        mesh=fine,
        in_specs=(
            nodes,
            P(),
            P(),
            nodes,
            P(row, col, None, None),
            P(row, col, None, None, None),
        ),
        out_specs=(nodes, nodes, P(), P()),
        check_vma=False,
    )
```

```python
import jax
import jax.numpy as jnp
import numpy as np
from jax import lax
from jax.experimental import pallas as pl
from jax.experimental.pallas import tpu as pltpu
from jax.sharding import Mesh
from jax.sharding import PartitionSpec as P

SIZES = {"x": 4, "yh": 2, "core": 2, "z": 8, "yl": 2}
AXES = tuple(SIZES)
PLANE = ("x", "yh")
F = 128
H = 256
TILE = 256
TMAX = 32
BLOCKS = 16
COUNT = 8
BLOCK = F + COUNT
SHARE = 16
PIECE = SHARE + 8
CUTS = (0, 8, 16, TMAX)
PARTS = len(CUTS) - 1
highest = lax.Precision.HIGHEST
f32 = jnp.float32
bf16 = jnp.bfloat16
together = lax.optimization_barrier


def shift(value, axis, by):
    size = SIZES[axis]
    return lax.ppermute(value, axis, [(i, (i + by) % size) for i in range(size)])


def params(mib):
    return pltpu.CompilerParams(vmem_limit_bytes=mib * 1024 * 1024)


def cost(tiles):
    return pl.CostEstimate(
        flops=4 * tiles * TILE * TILE * F, bytes_accessed=2 * TMAX * TILE * TILE, transcendentals=0
    )


def split_terms(values):
    high = values.astype(bf16)
    return high, (values - high.astype(f32)).astype(bf16)


def source_slot(block):
    x, yh, core = block >> 2, (block >> 1) & 1, block & 1
    x_rel = (x - lax.axis_index("x")) & 3
    yh_rel = yh ^ lax.axis_index("yh")
    core_rel = core ^ lax.axis_index("core")
    return core_rel * 8 + x_rel * 2 + yh_rel


def target_slot(block):
    z, yl = block >> 1, block & 1
    return ((z - lax.axis_index("z")) & 7) * 2 + (yl ^ lax.axis_index("yl"))


def over_tiles(mask_refs, use):
    for start, ref in zip(CUTS, mask_refs):
        for k in range(ref.shape[0]):
            use(start + k, ref[k].astype(f32).astype(bf16))


def forward_body(index_ref, *refs):
    masks, sources, (out_ref, held) = refs[:PARTS], refs[PARTS:-2], refs[-2:]
    for slot in range(BLOCKS):
        high, low = split_terms(sources[slot][...])
        held[slot, :F, :] = high
        held[slot, F : 2 * F, :] = low
        held[slot, 2 * F :, :] = jnp.ones((16, TILE), bf16)
    out_ref[...] = jnp.zeros_like(out_ref)

    def use(tile, mask):
        target = target_slot(index_ref[0, tile])
        source = source_slot(index_ref[1, tile])
        product = lax.dot_general(
            held[source], mask, (((1,), (1,)), ((), ())), preferred_element_type=f32
        )
        out_ref[target, :F, :] += product[:F] + product[F : 2 * F]
        out_ref[target, F:, :] += product[2 * F : 2 * F + COUNT]

    over_tiles(masks, use)


def vmem(count):
    return [pl.BlockSpec(memory_space=pltpu.SMEM)] + [pl.BlockSpec(memory_space=pltpu.VMEM)] * count


def forward_products(index, masks, sources):
    return pl.pallas_call(
        forward_body,
        in_specs=vmem(PARTS + BLOCKS),
        out_shape=jax.ShapeDtypeStruct((BLOCKS, BLOCK, TILE), f32),
        scratch_shapes=[pltpu.VMEM((BLOCKS, 2 * F + 16, TILE), bf16)],
        compiler_params=params(24),
        cost_estimate=cost(TMAX),
    )(index, *masks, *sources)


def dense_body(a_ref, b_ref, c_ref, d_ref, x_ref, w_ref, o_ref, g_ref, hidden_ref, out_ref, gw_ref):
    total = a_ref[...] + b_ref[...] + c_ref[...] + d_ref[...]
    degree = 1.0 + total[F : F + 1]
    aggregated = (total[:F] + x_ref[...]) / degree
    weight = w_ref[...]
    active = (
        jnp.dot(aggregated.T, weight, precision=highest, preferred_element_type=f32) + o_ref[...]
    )
    bell = 1.0 + lax.erf(active * 0.7071067811865476)
    hidden_ref[...] = 0.5 * active * bell
    slope = 0.5 * bell + active * jnp.exp(-0.5 * active * active) * 0.3989422804014327
    grad_pre = g_ref[...] * slope
    out_ref[...] = (
        lax.dot_general(
            weight, grad_pre, (((1,), (1,)), ((), ())), precision=highest, preferred_element_type=f32
        )
        / degree
    )
    gw_ref[:F, :] = jnp.dot(aggregated, grad_pre, precision=highest, preferred_element_type=f32)
    gw_ref[F:, :] = jnp.broadcast_to(jnp.sum(grad_pre, axis=0, keepdims=True), (8, H))


def dense(parts, x_t, weight, offset, cotangent):
    return pl.pallas_call(
        dense_body,
        out_shape=(
            jax.ShapeDtypeStruct((TILE, H), f32),
            jax.ShapeDtypeStruct((F, TILE), f32),
            jax.ShapeDtypeStruct((F + 8, H), f32),
        ),
        compiler_params=params(24),
    )(*parts, x_t, weight, offset.reshape(1, H), cotangent)


def backward_body(index_ref, *refs):
    masks, ins, (near_ref, far_ref, held, sums) = refs[:PARTS], refs[PARTS:-4], refs[-4:]
    places = [(0, 0), (7, 1), (1, 2), (6, 3), (2, 4), (5, 5), (3, 6)]
    parts = [(2 * z + h, ins[k], h * F) for z, k in places for h in range(2)]
    parts += [(8, ins[7], 0), (9, ins[8], 0)]
    for slot, ref, start in parts:
        high, low = split_terms(ref[start : start + F, :])
        held[slot, :F, :] = high
        held[slot, F:, :] = low
    sums[...] = jnp.zeros_like(sums)
    core = lax.axis_index("core")

    def use(tile, mask):
        source = target_slot(index_ref[0, tile])
        block = index_ref[1, tile]
        product = jnp.dot(held[source], mask, preferred_element_type=f32)
        sums[((block & 1) ^ core) * 8 + (block >> 1)] += product[:F] + product[F:]

    over_tiles(masks, use)
    near_ref[...] = sums[:8]
    far_ref[...] = sums[8:]


def backward_products(index, masks, gathered):
    half = jax.ShapeDtypeStruct((8, F, TILE), f32)
    return pl.pallas_call(
        backward_body,
        in_specs=vmem(PARTS + len(gathered)),
        out_shape=(half, half),
        scratch_shapes=[
            pltpu.VMEM((BLOCKS, 2 * F, TILE), bf16),
            pltpu.VMEM((BLOCKS, F, TILE), f32),
        ],
        compiler_params=params(24),
        cost_estimate=cost(TMAX),
    )(index, *masks, *gathered)


SCALE = 1.0 / float(np.sqrt(BLOCKS * BLOCKS * TILE))


def final_body(parts_ref, out_ref, piece_ref, grad_ref, gw_ref, go_ref):
    total = out_ref[...]
    for k in range(8):
        total = total + parts_ref[k, :F, :]
        gw_ref[k * SHARE : (k + 1) * SHARE, :] = parts_ref[k, F:, :] * SCALE
    grad_ref[...] = total.T
    go_ref[...] = piece_ref[SHARE : SHARE + 1, :] * SCALE


def finish(parts, outgoing, piece):
    return pl.pallas_call(
        final_body,
        out_shape=(
            jax.ShapeDtypeStruct((TILE, F), f32),
            jax.ShapeDtypeStruct((F, H), f32),
            jax.ShapeDtypeStruct((1, H), f32),
        ),
        compiler_params=params(16),
    )(parts, outgoing, piece)


def gather_row(x_t, mask):
    h = shift(x_t, "yh", 1)
    r1, l1 = shift(x_t, "x", 1), shift(x_t, "x", -1)
    narrow = lambda whole, k: whole[CUTS[k] : CUTS[k + 1]].astype(jnp.int8)
    m0 = narrow(mask, 0)
    h, m0, mask = together((h, m0, mask))
    r1h, l1h = shift(h, "x", 1), shift(h, "x", -1)
    m1 = narrow(mask, 1)
    l1h, m1, mask = together((l1h, m1, mask))
    r2, l2 = shift(r1, "x", 1), shift(l1h, "x", -1)
    l2, m2 = together((l2, narrow(mask, 2)))
    own = [x_t, h, l1, l1h, r2, l2, r1, r1h]
    pairs = [[x_t, h], [l1, r1], [l1h, r1h], [r2, l2]]
    far = []
    for a, b in pairs:
        both = shift(jnp.concatenate([a, b], axis=0), "core", 1)
        far.append((both[:F], both[F:]))
    (f0, f1), (f2, f6), (f3, f7), (f4, f5) = far
    return own + [f0, f1, f2, f3, f4, f5, f6, f7], (m0, m1, m2)


def scatter_col(sums):
    two = lambda z: sums[2 * (z % 8) : 2 * (z % 8) + 2].reshape(2 * BLOCK, TILE)
    right, left = shift(sums[8], "z", 1), shift(sums[9], "z", -1)
    right = two(3).at[:BLOCK].add(right)
    left = two(-3).at[BLOCK:].add(left)
    right, left = shift(right, "z", 1), shift(left, "z", -1)
    right, left = shift(right + two(2), "z", 1), shift(left + two(-2), "z", -1)
    right, left = shift(right + two(1), "z", 1), shift(left + two(-1), "z", -1)
    other = shift(right[BLOCK:] + left[BLOCK:] + sums[1], "yl", 1)
    return sums[0], right[:BLOCK], left[:BLOCK], other


def gather_col(value, gw):
    other, gw = together((shift(value, "yl", 1), gw + shift(gw, "core", 1)))
    both = jnp.concatenate([value, other], axis=0)
    shares = jnp.concatenate(
        [gw[:F].reshape(8, SHARE, H), jnp.broadcast_to(gw[F:], (8, 8, H))], axis=1
    )
    r1, l1, shares = together(
        (
            shift(both, "z", 1),
            shift(both, "z", -1),
            lax.all_to_all(shares, PLANE, 0, 0, tiled=True),
        )
    )
    piece = jnp.sum(shares, axis=0)
    r2 = shift(jnp.concatenate([r1, piece], axis=0), "z", 1)
    l2 = shift(jnp.concatenate([l1, piece], axis=0), "z", -1)
    r3, l3 = shift(r2, "z", 1), shift(l2, "z", -1)
    r4 = shift(jnp.concatenate([r3[:F], r3[2 * F :]], axis=0), "z", 1)
    l4 = shift(l3[F:], "z", -1)
    for ref, at in ((r2, 2 * F), (l2, 2 * F), (r3, 2 * F), (l3, 2 * F), (r4, F), (l4, F)):
        piece = piece + ref[at:]
    return (both, r1, l1, r2, l2, r3, l3, r4, l4), piece, r4[F:]


def scatter_row(index, masks, gathered, piece, last):
    (near, far), last = together((backward_products(index, masks, gathered), shift(last, "z", 1)))
    piece = piece + last
    got, piece = together((shift(far, "core", 1), piece + shift(piece, "yl", 1)))
    share = jnp.broadcast_to(piece[:SHARE], (8, SHARE, H))
    total = jnp.concatenate([near + got, share], axis=1)
    return lax.all_to_all(total, PLANE, 0, 0, tiled=True), piece


def per_device(features, weight, offset, cotangent, tile_index, edge_mask):
    index = tile_index.reshape(2, TMAX)
    x_t = features.T
    sources, masks = gather_row(x_t, edge_mask.reshape(TMAX, TILE, TILE))
    parts = scatter_col(forward_products(index, masks, sources))
    hidden, outgoing, gw = dense(parts, x_t, weight, offset, cotangent)
    gathered, piece, last = gather_col(outgoing, gw)
    parts, piece = scatter_row(index, masks, gathered, piece, last)
    grad, grad_weight, grad_offset = finish(parts, outgoing, piece)
    return hidden, grad, grad_weight, grad_offset.reshape(H)


def solution(mesh):
    fine = Mesh(mesh.devices.reshape(tuple(SIZES.values())), AXES)
    row, col = ("x", "yh", "core"), ("z", "yl")
    nodes = P(row + col, None)
    return jax.shard_map(
        per_device,
        mesh=fine,
        in_specs=(
            nodes,
            P(),
            P(),
            nodes,
            P(row, col, None, None),
            P(row, col, None, None, None),
        ),
        out_specs=(nodes, nodes, P(), P()),
        check_vma=False,
    )
```

```python
import jax
import jax.numpy as jnp
import numpy as np
from jax import lax
from jax.experimental import pallas as pl
from jax.experimental.pallas import tpu as pltpu
from jax.sharding import Mesh
from jax.sharding import PartitionSpec as P

SIZES = {"x": 4, "yh": 2, "core": 2, "z": 8, "yl": 2}
AXES = tuple(SIZES)
PLANE = ("x", "yh")
F = 128
H = 256
TILE = 256
TMAX = 32
BLOCKS = 16
COUNT = 8
BLOCK = F + COUNT
SHARE = 16
PIECE = SHARE + 8
PARTS = 8
LISTED = TMAX // PARTS
highest = lax.Precision.HIGHEST
f32 = jnp.float32
bf16 = jnp.bfloat16
together = lax.optimization_barrier


def shift(value, axis, by):
    size = SIZES[axis]
    return lax.ppermute(value, axis, [(i, (i + by) % size) for i in range(size)])


def params(mib):
    return pltpu.CompilerParams(vmem_limit_bytes=mib * 1024 * 1024)


def cost(tiles):
    return pl.CostEstimate(
        flops=4 * tiles * TILE * TILE * F, bytes_accessed=2 * TMAX * TILE * TILE, transcendentals=0
    )


def split_terms(values):
    high = values.astype(bf16)
    return high, (values - high.astype(f32)).astype(bf16)


def source_slot(block):
    x, yh, core = block >> 2, (block >> 1) & 1, block & 1
    x_rel = (x - lax.axis_index("x")) & 3
    yh_rel = yh ^ lax.axis_index("yh")
    core_rel = core ^ lax.axis_index("core")
    return core_rel * 8 + x_rel * 2 + yh_rel


def target_slot(block):
    z, yl = block >> 1, block & 1
    return ((z - lax.axis_index("z")) & 7) * 2 + (yl ^ lax.axis_index("yl"))


def widen(mask):
    return mask.astype(f32).astype(bf16)


def forward_body(index_ref, mask_ref, *refs):
    sources, (out_ref, narrow_ref, held, wide, arrived) = refs[:-5], refs[-5:]
    copies = []
    for part in range(PARTS):
        rows = pl.ds(part * LISTED, LISTED)
        copies.append(pltpu.make_async_copy(mask_ref.at[rows], wide.at[rows], arrived.at[part]))
        copies[-1].start()
    for slot in range(BLOCKS):
        high, low = split_terms(sources[slot][...])
        held[slot, :F, :] = high
        held[slot, F : 2 * F, :] = low
        held[slot, 2 * F :, :] = jnp.ones((16, TILE), bf16)
    out_ref[...] = jnp.zeros_like(out_ref)
    for tile in range(TMAX):
        if tile % LISTED == 0:
            copies[tile // LISTED].wait()
        target = target_slot(index_ref[0, tile])
        source = source_slot(index_ref[1, tile])
        mask = wide[tile]
        narrow_ref[tile] = mask.astype(jnp.int8)
        product = lax.dot_general(
            held[source], widen(mask), (((1,), (1,)), ((), ())), preferred_element_type=f32
        )
        out_ref[target, :F, :] += product[:F] + product[F : 2 * F]
        out_ref[target, F:, :] += product[2 * F : 2 * F + COUNT]


def vmem(count):
    return [pl.BlockSpec(memory_space=pltpu.VMEM)] * count


def forward_products(index, mask, sources):
    return pl.pallas_call(
        forward_body,
        in_specs=[pl.BlockSpec(memory_space=pltpu.SMEM), pl.BlockSpec(memory_space=pl.ANY)]
        + vmem(BLOCKS),
        out_specs=tuple(vmem(2)),
        out_shape=(
            jax.ShapeDtypeStruct((BLOCKS, BLOCK, TILE), f32),
            jax.ShapeDtypeStruct((TMAX, TILE, TILE), jnp.int8),
        ),
        scratch_shapes=[
            pltpu.VMEM((BLOCKS, 2 * F + 16, TILE), bf16),
            pltpu.VMEM((TMAX, TILE, TILE), jnp.int32),
            pltpu.SemaphoreType.DMA((PARTS,)),
        ],
        compiler_params=params(46),
        cost_estimate=cost(TMAX),
    )(index, mask, *sources)


def dense_body(a_ref, b_ref, c_ref, d_ref, x_ref, w_ref, o_ref, g_ref, hidden_ref, out_ref, gw_ref):
    total = a_ref[...] + b_ref[...] + c_ref[...] + d_ref[...]
    degree = 1.0 + total[F : F + 1]
    aggregated = (total[:F] + x_ref[...]) / degree
    weight = w_ref[...]
    active = (
        jnp.dot(aggregated.T, weight, precision=highest, preferred_element_type=f32) + o_ref[...]
    )
    bell = 1.0 + lax.erf(active * 0.7071067811865476)
    hidden_ref[...] = 0.5 * active * bell
    slope = 0.5 * bell + active * jnp.exp(-0.5 * active * active) * 0.3989422804014327
    grad_pre = g_ref[...] * slope
    out_ref[...] = (
        lax.dot_general(
            weight, grad_pre, (((1,), (1,)), ((), ())), precision=highest, preferred_element_type=f32
        )
        / degree
    )
    gw_ref[:F, :] = jnp.dot(aggregated, grad_pre, precision=highest, preferred_element_type=f32)
    gw_ref[F:, :] = jnp.broadcast_to(jnp.sum(grad_pre, axis=0, keepdims=True), (8, H))


def dense(parts, x_t, weight, offset, cotangent):
    return pl.pallas_call(
        dense_body,
        out_shape=(
            jax.ShapeDtypeStruct((TILE, H), f32),
            jax.ShapeDtypeStruct((F, TILE), f32),
            jax.ShapeDtypeStruct((F + 8, H), f32),
        ),
        compiler_params=params(24),
    )(*parts, x_t, weight, offset.reshape(1, H), cotangent)


def backward_body(index_ref, mask_ref, *refs):
    ins, (near_ref, far_ref, held, sums) = refs[:-4], refs[-4:]
    places = [(0, 0), (7, 1), (1, 2), (6, 3), (2, 4), (5, 5), (3, 6)]
    parts = [(2 * z + h, ins[k], h * F) for z, k in places for h in range(2)]
    parts += [(8, ins[7], 0), (9, ins[8], 0)]
    for slot, ref, start in parts:
        high, low = split_terms(ref[start : start + F, :])
        held[slot, :F, :] = high
        held[slot, F:, :] = low
    sums[...] = jnp.zeros_like(sums)
    core = lax.axis_index("core")
    for tile in range(TMAX):
        source = target_slot(index_ref[0, tile])
        block = index_ref[1, tile]
        product = jnp.dot(held[source], widen(mask_ref[tile]), preferred_element_type=f32)
        sums[((block & 1) ^ core) * 8 + (block >> 1)] += product[:F] + product[F:]
    near_ref[...] = sums[:8]
    far_ref[...] = sums[8:]


def backward_products(index, mask, gathered):
    half = jax.ShapeDtypeStruct((8, F, TILE), f32)
    return pl.pallas_call(
        backward_body,
        in_specs=[pl.BlockSpec(memory_space=pltpu.SMEM)] + vmem(1 + len(gathered)),
        out_shape=(half, half),
        scratch_shapes=[
            pltpu.VMEM((BLOCKS, 2 * F, TILE), bf16),
            pltpu.VMEM((BLOCKS, F, TILE), f32),
        ],
        compiler_params=params(24),
        cost_estimate=cost(TMAX),
    )(index, mask, *gathered)


SCALE = 1.0 / float(np.sqrt(BLOCKS * BLOCKS * TILE))


def final_body(parts_ref, out_ref, piece_ref, grad_ref, gw_ref, go_ref):
    total = out_ref[...]
    for k in range(8):
        total = total + parts_ref[k, :F, :]
        gw_ref[k * SHARE : (k + 1) * SHARE, :] = parts_ref[k, F:, :] * SCALE
    grad_ref[...] = total.T
    go_ref[...] = piece_ref[SHARE : SHARE + 1, :] * SCALE


def finish(parts, outgoing, piece):
    return pl.pallas_call(
        final_body,
        out_shape=(
            jax.ShapeDtypeStruct((TILE, F), f32),
            jax.ShapeDtypeStruct((F, H), f32),
            jax.ShapeDtypeStruct((1, H), f32),
        ),
        compiler_params=params(16),
    )(parts, outgoing, piece)


def gather_row(x_t):
    h = shift(x_t, "yh", 1)
    r1, l1 = shift(x_t, "x", 1), shift(x_t, "x", -1)
    r1h, l1h = shift(h, "x", 1), shift(h, "x", -1)
    r2, l2 = shift(r1, "x", 1), shift(l1h, "x", -1)
    own = [x_t, h, l1, l1h, r2, l2, r1, r1h]
    pairs = [[x_t, h], [l1, r1], [l1h, r1h], [r2, l2]]
    far = []
    for a, b in pairs:
        both = shift(jnp.concatenate([a, b], axis=0), "core", 1)
        far.append((both[:F], both[F:]))
    (f0, f1), (f2, f6), (f3, f7), (f4, f5) = far
    return own + [f0, f1, f2, f3, f4, f5, f6, f7]


def scatter_col(sums):
    two = lambda z: sums[2 * (z % 8) : 2 * (z % 8) + 2].reshape(2 * BLOCK, TILE)
    right, left = shift(sums[8], "z", 1), shift(sums[9], "z", -1)
    right = two(3).at[:BLOCK].add(right)
    left = two(-3).at[BLOCK:].add(left)
    right, left = shift(right, "z", 1), shift(left, "z", -1)
    right, left = shift(right + two(2), "z", 1), shift(left + two(-2), "z", -1)
    right, left = shift(right + two(1), "z", 1), shift(left + two(-1), "z", -1)
    other = shift(right[BLOCK:] + left[BLOCK:] + sums[1], "yl", 1)
    return sums[0], right[:BLOCK], left[:BLOCK], other


def gather_col(value, gw):
    other, gw = together((shift(value, "yl", 1), gw + shift(gw, "core", 1)))
    both = jnp.concatenate([value, other], axis=0)
    shares = jnp.concatenate(
        [gw[:F].reshape(8, SHARE, H), jnp.broadcast_to(gw[F:], (8, 8, H))], axis=1
    )
    r1, l1, shares = together(
        (
            shift(both, "z", 1),
            shift(both, "z", -1),
            lax.all_to_all(shares, PLANE, 0, 0, tiled=True),
        )
    )
    piece = jnp.sum(shares, axis=0)
    r2 = shift(jnp.concatenate([r1, piece], axis=0), "z", 1)
    l2 = shift(jnp.concatenate([l1, piece], axis=0), "z", -1)
    r3, l3 = shift(r2, "z", 1), shift(l2, "z", -1)
    r4 = shift(jnp.concatenate([r3[:F], r3[2 * F :]], axis=0), "z", 1)
    l4 = shift(l3[F:], "z", -1)
    for ref, at in ((r2, 2 * F), (l2, 2 * F), (r3, 2 * F), (l3, 2 * F), (r4, F), (l4, F)):
        piece = piece + ref[at:]
    return (both, r1, l1, r2, l2, r3, l3, r4, l4), piece, r4[F:]


def scatter_row(index, mask, gathered, piece, last):
    (near, far), last = together((backward_products(index, mask, gathered), shift(last, "z", 1)))
    piece = piece + last
    got, piece = together((shift(far, "core", 1), piece + shift(piece, "yl", 1)))
    share = jnp.broadcast_to(piece[:SHARE], (8, SHARE, H))
    total = jnp.concatenate([near + got, share], axis=1)
    return lax.all_to_all(total, PLANE, 0, 0, tiled=True), piece


def per_device(features, weight, offset, cotangent, tile_index, edge_mask):
    index = tile_index.reshape(2, TMAX)
    x_t = features.T
    mask = edge_mask.reshape(TMAX, TILE, TILE)
    sums, mask = forward_products(index, mask, gather_row(x_t))
    parts = scatter_col(sums)
    hidden, outgoing, gw = dense(parts, x_t, weight, offset, cotangent)
    gathered, piece, last = gather_col(outgoing, gw)
    parts, piece = scatter_row(index, mask, gathered, piece, last)
    grad, grad_weight, grad_offset = finish(parts, outgoing, piece)
    return hidden, grad, grad_weight, grad_offset.reshape(H)


def solution(mesh):
    fine = Mesh(mesh.devices.reshape(tuple(SIZES.values())), AXES)
    row, col = ("x", "yh", "core"), ("z", "yl")
    nodes = P(row + col, None)
    return jax.shard_map(
        per_device,
        mesh=fine,
        in_specs=(
            nodes,
            P(),
            P(),
            nodes,
            P(row, col, None, None),
            P(row, col, None, None, None),
        ),
        out_specs=(nodes, nodes, P(), P()),
        check_vma=False,
    )
```

```python
import jax
import jax.numpy as jnp
import numpy as np
from jax import lax
from jax.experimental import pallas as pl
from jax.experimental.pallas import tpu as pltpu
from jax.sharding import Mesh
from jax.sharding import PartitionSpec as P

SIZES = {"x": 4, "yh": 2, "core": 2, "z": 8, "yl": 2}
AXES = tuple(SIZES)
PLANE = ("x", "yh")
F = 128
H = 256
TILE = 256
TMAX = 32
BLOCKS = 16
COUNT = 8
BLOCK = F + COUNT
SHARE = 16
PIECE = SHARE + 8
PARTS = 8
LISTED = TMAX // PARTS
f32 = jnp.float32
bf16 = jnp.bfloat16
together = lax.optimization_barrier


def shift(value, axis, by):
    size = SIZES[axis]
    return lax.ppermute(value, axis, [(i, (i + by) % size) for i in range(size)])


def params(mib):
    return pltpu.CompilerParams(vmem_limit_bytes=mib * 1024 * 1024)


def cost(tiles):
    return pl.CostEstimate(
        flops=4 * tiles * TILE * TILE * F, bytes_accessed=2 * TMAX * TILE * TILE, transcendentals=0
    )


def split_terms(values):
    high = values.astype(bf16)
    return high, (values - high.astype(f32)).astype(bf16)


def source_slot(block):
    x, yh, core = block >> 2, (block >> 1) & 1, block & 1
    x_rel = (x - lax.axis_index("x")) & 3
    yh_rel = yh ^ lax.axis_index("yh")
    core_rel = core ^ lax.axis_index("core")
    return core_rel * 8 + x_rel * 2 + yh_rel


def target_slot(block):
    z, yl = block >> 1, block & 1
    return ((z - lax.axis_index("z")) & 7) * 2 + (yl ^ lax.axis_index("yl"))


def widen(mask):
    return mask.astype(f32).astype(bf16)


def forward_body(index_ref, mask_ref, *refs):
    sources, (out_ref, narrow_ref, held, wide, arrived) = refs[:-5], refs[-5:]
    copies = []
    for part in range(PARTS):
        rows = pl.ds(part * LISTED, LISTED)
        copies.append(pltpu.make_async_copy(mask_ref.at[rows], wide.at[rows], arrived.at[part]))
        copies[-1].start()
    for slot in range(BLOCKS):
        high, low = split_terms(sources[slot][...])
        held[slot, :F, :] = high
        held[slot, F : 2 * F, :] = low
        held[slot, 2 * F :, :] = jnp.ones((16, TILE), bf16)
    out_ref[...] = jnp.zeros_like(out_ref)
    for tile in range(TMAX):
        if tile % LISTED == 0:
            copies[tile // LISTED].wait()
        target = target_slot(index_ref[0, tile])
        source = source_slot(index_ref[1, tile])
        mask = wide[tile]
        narrow_ref[tile] = mask.astype(jnp.int8)
        product = lax.dot_general(
            held[source], widen(mask), (((1,), (1,)), ((), ())), preferred_element_type=f32
        )
        out_ref[target, :F, :] += product[:F] + product[F : 2 * F]
        out_ref[target, F:, :] += product[2 * F : 2 * F + COUNT]


def vmem(count):
    return [pl.BlockSpec(memory_space=pltpu.VMEM)] * count


def forward_products(index, mask, sources):
    return pl.pallas_call(
        forward_body,
        in_specs=[pl.BlockSpec(memory_space=pltpu.SMEM), pl.BlockSpec(memory_space=pl.ANY)]
        + vmem(BLOCKS),
        out_specs=tuple(vmem(2)),
        out_shape=(
            jax.ShapeDtypeStruct((BLOCKS, BLOCK, TILE), f32),
            jax.ShapeDtypeStruct((TMAX, TILE, TILE), jnp.int8),
        ),
        scratch_shapes=[
            pltpu.VMEM((BLOCKS, 2 * F + 16, TILE), bf16),
            pltpu.VMEM((TMAX, TILE, TILE), jnp.int32),
            pltpu.SemaphoreType.DMA((PARTS,)),
        ],
        compiler_params=params(46),
        cost_estimate=cost(TMAX),
    )(index, mask, *sources)


def product(left, right, dims):
    left_high, left_low = split_terms(left)
    right_high, right_low = split_terms(right)
    dot = lambda a, b: lax.dot_general(a, b, (dims, ((), ())), preferred_element_type=f32)
    return dot(left_high, right_high) + (dot(left_high, right_low) + dot(left_low, right_high))


def dense_body(a_ref, b_ref, c_ref, d_ref, x_ref, w_ref, o_ref, g_ref, hidden_ref, out_ref, gw_ref):
    total = a_ref[...] + b_ref[...] + c_ref[...] + d_ref[...]
    degree = 1.0 + total[F : F + 1]
    aggregated = (total[:F] + x_ref[...]) / degree
    weight = w_ref[...]
    active = product(aggregated.T, weight, ((1,), (0,))) + o_ref[...]
    bell = 1.0 + lax.erf(active * 0.7071067811865476)
    hidden_ref[...] = 0.5 * active * bell
    slope = 0.5 * bell + active * jnp.exp(-0.5 * active * active) * 0.3989422804014327
    grad_pre = g_ref[...] * slope
    out_ref[...] = product(weight, grad_pre, ((1,), (1,))) / degree
    gw_ref[:F, :] = product(aggregated, grad_pre, ((1,), (0,)))
    gw_ref[F:, :] = jnp.broadcast_to(jnp.sum(grad_pre, axis=0, keepdims=True), (8, H))


def dense(parts, x_t, weight, offset, cotangent):
    return pl.pallas_call(
        dense_body,
        out_shape=(
            jax.ShapeDtypeStruct((TILE, H), f32),
            jax.ShapeDtypeStruct((F, TILE), f32),
            jax.ShapeDtypeStruct((F + 8, H), f32),
        ),
        compiler_params=params(24),
    )(*parts, x_t, weight, offset.reshape(1, H), cotangent)


def backward_body(index_ref, mask_ref, *refs):
    ins, (near_ref, far_ref, held, sums) = refs[:-4], refs[-4:]
    places = [(0, 0), (7, 1), (1, 2), (6, 3), (2, 4), (5, 5), (3, 6)]
    parts = [(2 * z + h, ins[k], h * F) for z, k in places for h in range(2)]
    parts += [(8, ins[7], 0), (9, ins[8], 0)]
    for slot, ref, start in parts:
        high, low = split_terms(ref[start : start + F, :])
        held[slot, :F, :] = high
        held[slot, F:, :] = low
    sums[...] = jnp.zeros_like(sums)
    core = lax.axis_index("core")
    for tile in range(TMAX):
        source = target_slot(index_ref[0, tile])
        block = index_ref[1, tile]
        product = jnp.dot(held[source], widen(mask_ref[tile]), preferred_element_type=f32)
        sums[((block & 1) ^ core) * 8 + (block >> 1)] += product[:F] + product[F:]
    near_ref[...] = sums[:8]
    far_ref[...] = sums[8:]


def backward_products(index, mask, gathered):
    half = jax.ShapeDtypeStruct((8, F, TILE), f32)
    return pl.pallas_call(
        backward_body,
        in_specs=[pl.BlockSpec(memory_space=pltpu.SMEM)] + vmem(1 + len(gathered)),
        out_shape=(half, half),
        scratch_shapes=[
            pltpu.VMEM((BLOCKS, 2 * F, TILE), bf16),
            pltpu.VMEM((BLOCKS, F, TILE), f32),
        ],
        compiler_params=params(24),
        cost_estimate=cost(TMAX),
    )(index, mask, *gathered)


SCALE = 1.0 / float(np.sqrt(BLOCKS * BLOCKS * TILE))


def final_body(parts_ref, out_ref, piece_ref, grad_ref, gw_ref, go_ref):
    total = out_ref[...]
    for k in range(8):
        total = total + parts_ref[k, :F, :]
        gw_ref[k * SHARE : (k + 1) * SHARE, :] = parts_ref[k, F:, :] * SCALE
    grad_ref[...] = total.T
    go_ref[...] = piece_ref[SHARE : SHARE + 1, :] * SCALE


def finish(parts, outgoing, piece):
    return pl.pallas_call(
        final_body,
        out_shape=(
            jax.ShapeDtypeStruct((TILE, F), f32),
            jax.ShapeDtypeStruct((F, H), f32),
            jax.ShapeDtypeStruct((1, H), f32),
        ),
        compiler_params=params(16),
    )(parts, outgoing, piece)


def gather_row(x_t):
    h = shift(x_t, "yh", 1)
    r1, l1 = shift(x_t, "x", 1), shift(x_t, "x", -1)
    r1h, l1h = shift(h, "x", 1), shift(h, "x", -1)
    r2, l2 = shift(r1, "x", 1), shift(l1h, "x", -1)
    own = [x_t, h, l1, l1h, r2, l2, r1, r1h]
    pairs = [[x_t, h], [l1, r1], [l1h, r1h], [r2, l2]]
    far = []
    for a, b in pairs:
        both = shift(jnp.concatenate([a, b], axis=0), "core", 1)
        far.append((both[:F], both[F:]))
    (f0, f1), (f2, f6), (f3, f7), (f4, f5) = far
    return own + [f0, f1, f2, f3, f4, f5, f6, f7]


def scatter_col(sums):
    two = lambda z: sums[2 * (z % 8) : 2 * (z % 8) + 2].reshape(2 * BLOCK, TILE)
    right, left = shift(sums[8], "z", 1), shift(sums[9], "z", -1)
    right = two(3).at[:BLOCK].add(right)
    left = two(-3).at[BLOCK:].add(left)
    right, left = shift(right, "z", 1), shift(left, "z", -1)
    right, left = shift(right + two(2), "z", 1), shift(left + two(-2), "z", -1)
    right, left = shift(right + two(1), "z", 1), shift(left + two(-1), "z", -1)
    other = shift(right[BLOCK:] + left[BLOCK:] + sums[1], "yl", 1)
    return sums[0], right[:BLOCK], left[:BLOCK], other


def gather_col(value, gw):
    other, gw = together((shift(value, "yl", 1), gw + shift(gw, "core", 1)))
    both = jnp.concatenate([value, other], axis=0)
    shares = jnp.concatenate(
        [gw[:F].reshape(8, SHARE, H), jnp.broadcast_to(gw[F:], (8, 8, H))], axis=1
    )
    r1, l1, shares = together(
        (
            shift(both, "z", 1),
            shift(both, "z", -1),
            lax.all_to_all(shares, PLANE, 0, 0, tiled=True),
        )
    )
    piece = jnp.sum(shares, axis=0)
    r2 = shift(jnp.concatenate([r1, piece], axis=0), "z", 1)
    l2 = shift(jnp.concatenate([l1, piece], axis=0), "z", -1)
    r3, l3 = shift(r2, "z", 1), shift(l2, "z", -1)
    r4 = shift(jnp.concatenate([r3[:F], r3[2 * F :]], axis=0), "z", 1)
    l4 = shift(l3[F:], "z", -1)
    for ref, at in ((r2, 2 * F), (l2, 2 * F), (r3, 2 * F), (l3, 2 * F), (r4, F), (l4, F)):
        piece = piece + ref[at:]
    return (both, r1, l1, r2, l2, r3, l3, r4, l4), piece, r4[F:]


def scatter_row(index, mask, gathered, piece, last):
    (near, far), last = together((backward_products(index, mask, gathered), shift(last, "z", 1)))
    piece = piece + last
    got, piece = together((shift(far, "core", 1), piece + shift(piece, "yl", 1)))
    share = jnp.broadcast_to(piece[:SHARE], (8, SHARE, H))
    total = jnp.concatenate([near + got, share], axis=1)
    return lax.all_to_all(total, PLANE, 0, 0, tiled=True), piece


def per_device(features, weight, offset, cotangent, tile_index, edge_mask):
    index = tile_index.reshape(2, TMAX)
    x_t = features.T
    mask = edge_mask.reshape(TMAX, TILE, TILE)
    sums, mask = forward_products(index, mask, gather_row(x_t))
    parts = scatter_col(sums)
    hidden, outgoing, gw = dense(parts, x_t, weight, offset, cotangent)
    gathered, piece, last = gather_col(outgoing, gw)
    parts, piece = scatter_row(index, mask, gathered, piece, last)
    grad, grad_weight, grad_offset = finish(parts, outgoing, piece)
    return hidden, grad, grad_weight, grad_offset.reshape(H)


def solution(mesh):
    fine = Mesh(mesh.devices.reshape(tuple(SIZES.values())), AXES)
    row, col = ("x", "yh", "core"), ("z", "yl")
    nodes = P(row + col, None)
    return jax.shard_map(
        per_device,
        mesh=fine,
        in_specs=(
            nodes,
            P(),
            P(),
            nodes,
            P(row, col, None, None),
            P(row, col, None, None, None),
        ),
        out_specs=(nodes, nodes, P(), P()),
        check_vma=False,
    )
```
